32 devices in a mesh: groups: 2 (over y), src: 4 (over z), tgt: 2 (over x), dir: 2 (over core).
Axes of the slice: x: 2, y: 2, z: 4, core: 2. Of those that a mesh axis runs over, the one named last changes fastest.
Arguments:
- incident: bfloat16 [2, 64, 4096], P(None, 'dir', ('groups', 'src')), parts along dimension 2, may hold values from -6 to 6
- near_blocks: bfloat16 [8, 2, 56, 2, 128, 128], P(('groups', 'src'), 'tgt'), parts along dimension 0, may hold values from -0.25 to 0.25
- near_src: int32 [8, 2, 56], P(('groups', 'src'), 'tgt'), parts along dimension 0, may hold values from 0 to 3
- near_tgt: int32 [8, 2, 56], P(('groups', 'src'), 'tgt'), parts along dimension 0, may hold values from 0 to 15, as said below
- far_v: bfloat16 [8, 2, 32, 2, 32, 128], P(('groups', 'src'), 'tgt'), parts along dimension 0, may hold values from -0.5 to 0.5
- far_src: int32 [8, 2, 32], P(('groups', 'src'), 'tgt'), parts along dimension 0, may hold values from 0 to 3
- far_dst: int32 [8, 2, 32], P(('groups', 'src'), 'tgt'), parts along dimension 0, may hold values from 0 to 127, as said below
- far_u: bfloat16 [8, 2, 32, 2, 32, 128], P(('groups', 'src'), 'tgt'), parts along dimension 0, may hold values from -0.75 to 0.75
- far_tgt: int32 [8, 2, 32], P(('groups', 'src'), 'tgt'), parts along dimension 0, may hold values from 0 to 3
Outputs:
- potential: float32 [2, 64, 4096], P(None, 'dir', ('groups', 'src', 'tgt')), parts along dimension 2
The draws below stay inside these ranges and needn't reach their ends.
There are 2 independent parts, one for each index of `groups`. The reference program is written for one: setup_inputs(seed, part) draws one part's arguments, and reference() takes and returns one part's arrays. A program takes and returns all parts, laid end to end along the dimension named above; each array names one. Nothing has to cross between parts.
Inputs may be any that keep to these rules, and one draw needn't show every extreme that they name: Near block (s, t, b) aims at owner near_tgt // 4. The near blocks of one device aimed at one owner other than s number at most 2 and reach at most 1 distinct target cluster; in every draw some owner receives exactly 2 near blocks from every device of every other owner. `far_dst`: value v names owner v // 32 and slot v % 32 at the same tgt index. Among the devices of one tgt index every value occurs exactly once; one device sends exactly 8 far blocks or none to each owner.
All inputs are finite; a program needn't handle non-finite values.
Results may differ from the reference program's by a relative error of at most 0.0025.
Values may be sent and summed in bfloat16 or wider, within the bound.
A program may use at most 64 MiB of HBM per device.

```python
import jax
import jax.numpy as jnp
from jax import lax

DIRS = 64
PANEL = 128
RANK = 32
NB_DEV = 56
FB_DEV = 32
CAP = 2
OWNERS = 4
QUARTERS = 2
CL_SRC = 4
CLUSTERS = 16
PANELS = 2048
CAPF = 8


def draw_near_tgt(key, part):
    hot_key, pool_key, order_key, contact_key, anywhere_key = jax.random.split(jax.random.fold_in(key, 11), 5)
    hot_owner = jax.random.randint(hot_key, (), 0, OWNERS)
    owner_ids = jnp.arange(OWNERS, dtype=jnp.int32)[:, None, None]
    hot_for = jnp.where(owner_ids == hot_owner, (hot_owner + 1) % OWNERS, hot_owner)
    width = NB_DEV + OWNERS * CAP
    self_part = jnp.broadcast_to(owner_ids, (OWNERS, QUARTERS, NB_DEV))
    other_part = jnp.broadcast_to((jnp.arange(OWNERS * CAP, dtype=jnp.int32) // CAP)[None, None, :], (OWNERS, QUARTERS, OWNERS * CAP))
    candidates = jnp.concatenate([self_part, other_part], axis=2)
    other_ok = (other_part != owner_ids) & (other_part != hot_for)
    usable = jnp.concatenate([jnp.ones((OWNERS, QUARTERS, NB_DEV), dtype=bool), other_ok], axis=2)
    position = jnp.arange(width, dtype=jnp.int32)[None, None, :]
    scores = jax.random.randint(pool_key, (OWNERS, QUARTERS, width), 0, 2 ** 20) * width + position
    scores = jnp.where(usable, scores, 2 ** 20 * width + position)
    taken = jnp.argsort(scores, axis=2)[:, :, :NB_DEV - CAP]
    picked = jnp.take_along_axis(candidates, taken, axis=2)
    destination = jnp.concatenate([jnp.broadcast_to(hot_for, (OWNERS, QUARTERS, CAP)), picked], axis=2)
    shuffle = jnp.argsort(jax.random.randint(order_key, (OWNERS, QUARTERS, NB_DEV), 0, 2 ** 20) * NB_DEV + jnp.arange(NB_DEV, dtype=jnp.int32)[None, None, :], axis=2)
    destination = jnp.take_along_axis(destination, shuffle, axis=2)
    contact = jax.random.randint(contact_key, (OWNERS, QUARTERS, OWNERS), 0, CL_SRC)
    aimed_at = jnp.take_along_axis(contact, destination, axis=2)
    anywhere = jax.random.randint(anywhere_key, (OWNERS, QUARTERS, NB_DEV), 0, CL_SRC)
    cluster = jnp.where(destination == owner_ids, anywhere, aimed_at)
    return (destination * CL_SRC + cluster).astype(jnp.int32)


def draw_far_dst(key, part):
    route_key, slot_key, order_key = jax.random.split(jax.random.fold_in(key, 23), 3)
    routes = jax.vmap(lambda sub_key: jax.random.permutation(sub_key, OWNERS))(jax.random.split(route_key, QUARTERS))
    slot_perm = jax.vmap(lambda sub_key: jax.random.permutation(sub_key, FB_DEV))(jax.random.split(slot_key, OWNERS * QUARTERS))
    slot_perm = slot_perm.reshape(OWNERS, QUARTERS, FB_DEV)
    owner_ids = jnp.arange(OWNERS, dtype=jnp.int32)[:, None, None]
    quarter_ids = jnp.arange(QUARTERS, dtype=jnp.int32)[None, :, None]
    item_ids = jnp.arange(FB_DEV, dtype=jnp.int32)[None, None, :]
    owner_of = routes[quarter_ids, (owner_ids + item_ids // CAPF) % OWNERS]
    encoded = owner_of * FB_DEV + slot_perm[owner_of, quarter_ids, item_ids]
    reorder = jnp.argsort(jax.random.randint(order_key, (OWNERS, QUARTERS, FB_DEV), 0, 2 ** 20) * FB_DEV + item_ids, axis=2)
    return jnp.take_along_axis(encoded, reorder, axis=2).astype(jnp.int32)


def plant(drawn, stream_key, low, largest):
    dims = drawn.shape
    spot = [jax.random.randint(jax.random.fold_in(stream_key, axis), (), 0, dims[axis]) for axis in range(len(dims))]
    drawn = drawn.at[tuple(spot)].set(low)
    longest = dims.index(max(dims))
    spot[longest] = (spot[longest] + 1) % dims[longest]
    return drawn.at[tuple(spot)].set(largest)


def steps_of(key, extent, shards, smallest, high):
    factor_of, own = 1.0, jax.random.fold_in(key, 6)
    for axis_at, parts in shards:
        draws = jnp.exp(jax.random.uniform(jax.random.fold_in(own, axis_at), (parts,), jnp.float32, smallest / len(shards), high / len(shards)))
        factor_of = factor_of * jnp.repeat(draws, extent[axis_at] // parts).reshape([-1 if axis == axis_at else 1 for axis in range(len(extent))])
    return factor_of


def centred(own_key, extent, spread, bound, cuts=(), held_as=jnp.bfloat16):
    array = spread * jax.random.normal(own_key, extent, jnp.float32)
    if cuts:
        array = array * steps_of(own_key, extent, cuts, -0.22, 0.18)
    return jnp.clip(array, -bound, bound).astype(held_as)


def setup_inputs(seed: int = 0, part: int = 0) -> dict:
    key_of = jax.random.split(jax.random.key(seed), 10)
    part_splits = jax.random.split(jax.random.fold_in(key_of[9], part), 10)
    return {
        "incident": centred(part_splits[0], (2, DIRS, PANELS), 1.0, 6.0, ((1, 2), (2, 4))),
        "near_blocks": centred(part_splits[1], (OWNERS, QUARTERS, NB_DEV, 2, PANEL, PANEL), (4 * PANEL) ** -0.5, 0.25, ((0, 4), (1, 2))),
        "near_src": plant(jax.random.randint(part_splits[2], (OWNERS, QUARTERS, NB_DEV), 0, CL_SRC), jax.random.fold_in(part_splits[2], 1), 0, CL_SRC - 1).astype(jnp.int32),
        "near_tgt": draw_near_tgt(jax.random.fold_in(jax.random.fold_in(key_of[9], part), 71), part),
        "far_v": centred(part_splits[4], (OWNERS, QUARTERS, FB_DEV, 2, RANK, PANEL), PANEL ** -0.5, 0.5, ((0, 4), (1, 2))),
        "far_src": plant(jax.random.randint(part_splits[5], (OWNERS, QUARTERS, FB_DEV), 0, CL_SRC), jax.random.fold_in(part_splits[5], 1), 0, CL_SRC - 1).astype(jnp.int32),
        "far_dst": draw_far_dst(jax.random.fold_in(jax.random.fold_in(key_of[9], part), 71), part),
        "far_u": centred(part_splits[7], (OWNERS, QUARTERS, FB_DEV, 2, RANK, PANEL), (2 * RANK) ** -0.5, 0.75, ((0, 4), (1, 2))),
        "far_tgt": plant(jax.random.randint(part_splits[8], (OWNERS, QUARTERS, FB_DEV), 0, CL_SRC), jax.random.fold_in(part_splits[8], 1), 0, CL_SRC - 1).astype(jnp.int32),
    }


def complex_apply(operand, matrices, pattern):
    products = jnp.einsum(pattern, operand.astype(jnp.float32), matrices.astype(jnp.float32), precision=lax.Precision.HIGHEST)
    return jnp.stack([products[:, 0, 0] - products[:, 1, 1], products[:, 1, 0] + products[:, 0, 1]], axis=1)


def reference(incident, near_blocks, near_src, near_tgt, far_v, far_src, far_dst, far_u, far_tgt):
    source = incident.reshape(2, DIRS, OWNERS, CL_SRC, PANEL)
    owner_ids = jnp.arange(OWNERS, dtype=jnp.int32)

    def near_step(cluster_total, owner_index):
        blocks = near_blocks[owner_index].reshape(QUARTERS * NB_DEV, 2, PANEL, PANEL)
        picked = jnp.take(source[:, :, owner_index], near_src[owner_index].reshape(-1).astype(jnp.int32), axis=2)
        partial_value = complex_apply(picked, blocks, "adbq,bcpq->bacdp")
        return cluster_total.at[near_tgt[owner_index].reshape(-1).astype(jnp.int32)].add(partial_value), None

    cluster_total = jnp.zeros((CLUSTERS, 2, DIRS, PANEL), jnp.float32)
    cluster_total, unused_near = lax.scan(near_step, cluster_total, owner_ids)

    def coeff_step(carried, owner_index):
        picked = jnp.take(source[:, :, owner_index], far_src[owner_index].reshape(-1).astype(jnp.int32), axis=2)
        factors = far_v[owner_index].reshape(QUARTERS * FB_DEV, 2, RANK, PANEL)
        coeffs = complex_apply(picked, factors, "adbq,bckq->bacdk").astype(jnp.bfloat16)
        return carried, coeffs.reshape(QUARTERS, FB_DEV, 2, DIRS, RANK)

    unused_carry, coefficients = lax.scan(coeff_step, jnp.zeros((), jnp.float32), owner_ids)
    quarter_ids = jnp.broadcast_to(jnp.arange(QUARTERS, dtype=jnp.int32)[None, :, None], far_dst.shape)
    arranged = jnp.zeros((QUARTERS, OWNERS * FB_DEV, 2, DIRS, RANK), coefficients.dtype)
    arranged = arranged.at[quarter_ids, far_dst.astype(jnp.int32)].set(coefficients)
    arranged = arranged.reshape(QUARTERS, OWNERS, FB_DEV, 2, DIRS, RANK).transpose(1, 0, 2, 3, 4, 5)

    def far_step(cluster_total, owner_index):
        factors = far_u[owner_index].reshape(QUARTERS * FB_DEV, 2, RANK, PANEL)
        coeffs = arranged[owner_index].reshape(QUARTERS * FB_DEV, 2, DIRS, RANK)
        potential = complex_apply(coeffs, factors, "badk,bckp->bacdp")
        clusters = owner_index * CL_SRC + far_tgt[owner_index].reshape(-1).astype(jnp.int32)
        return cluster_total.at[clusters].add(potential), None

    cluster_total, unused_far = lax.scan(far_step, cluster_total, owner_ids)
    return cluster_total.transpose(1, 2, 0, 3).reshape(2, DIRS, PANELS)
```

```python
import functools

import jax
import jax.numpy as jnp
from jax import lax
from jax.experimental import pallas as pl
from jax.experimental.pallas import tpu as pltpu
from jax.sharding import PartitionSpec as P

PANEL = 128
CHUNK = 8
MESH = pl.DeviceIdType.MESH
F32 = jnp.float32
BF16 = jnp.bfloat16
I32 = jnp.int32

PERM, PREV, LAST, SLOT, CLUSTER = range(5)


def shift_of(size):
    assert size & (size - 1) == 0
    return size.bit_length() - 1


def loop(start, stop, step):
    if stop - start <= 8:
        for index in range(start, stop):
            step(index)
    else:

        @pl.loop(start, stop)
        def _(index):
            step(index)


def iota(shape, axis):
    return lax.broadcasted_iota(I32, shape, axis)


def column(row):
    size = row.shape[1]
    eye = iota((size, size), 0) == iota((size, size), 1)
    return jnp.sum(jnp.where(eye, row, 0.0), axis=1, keepdims=True)


def dot_nt(left, right):
    return lax.dot_general(left, right, (((1,), (1,)), ((), ())), preferred_element_type=F32)


def offset_row(owner, me, owners):
    offset = owner - me
    return jnp.where(offset < 0, offset + owners, offset)


def kernel(
    owners, tgts, depth,
    inc_h, nb_h, nsrc, ntgt, fv_h, fsrc, fdst, fu_h, ftgt,
    out_ref,
    inc, nb, fv, fu, stacked, tab, tab_in, tab_s, far_out, far_in, run, near_out, near_in, acc,
    tg_out, tg_in,
    in_sem, nb_sem, tab_sem, lab_send, lab_recv, far_send, far_recv, near_send, near_recv,
    tg_send, tg_recv,
):
    count, half = nb.shape[0], inc.shape[1]
    clusters = inc.shape[2] // PANEL
    far_count, rank = fv.shape[0], fv.shape[2]
    width = depth * rank
    share = clusters // tgts
    me, mine = lax.axis_index("src"), lax.axis_index("tgt")

    def read(step, row, lane, top):
        return jnp.clip(tab_s[step, row, lane], 0, top)

    def owner_at(step):
        return lax.rem(me + step, owners)

    def tgt_at(step):
        return lax.rem(mine + step, tgts)

    barrier = pltpu.get_barrier_semaphore()

    def greet_owner(step):
        pl.semaphore_signal(barrier, inc=1, device_id={"src": owner_at(step)}, device_id_type=MESH)

    def greet_tgt(step):
        pl.semaphore_signal(barrier, inc=1, device_id={"tgt": tgt_at(step)}, device_id_type=MESH)

    loop(1, owners, greet_owner)
    loop(1, tgts, greet_tgt)

    load_inc = pltpu.make_async_copy(inc_h.at[...], inc, in_sem.at[0])
    load_fv = pltpu.make_async_copy(fv_h.at[0, 0], fv, in_sem.at[1])
    load_fu = pltpu.make_async_copy(fu_h.at[0, 0], fu, in_sem.at[2])
    load_inc.start()
    load_fv.start()

    def load_nb(chunk):
        part = pl.ds(chunk * CHUNK, CHUNK)
        return pltpu.make_async_copy(nb_h.at[0, 0, part], nb.at[part], nb_sem.at[chunk])

    for chunk in range(count // CHUNK):
        load_nb(chunk).start()
    load_fu.start()

    target = ntgt[0]
    own_bits = shift_of(clusters)
    step_row = offset_row(lax.shift_right_logical(target, own_bits), me, owners)
    local_row = target & (clusters - 1)
    bucket_row = jnp.where(step_row == 0, local_row, clusters + step_row - 1).astype(F32)
    bucket_col = column(bucket_row)
    local_col = column(local_row.astype(F32))
    at0, at1 = iota((count, count), 0), iota((count, count), 1)
    before = (bucket_col == bucket_row) & (at0 < at1)
    prev = jnp.max(jnp.where(before, at0.astype(F32), -1.0), axis=0, keepdims=True)
    prev = jnp.where(prev < 0, float(count), prev)
    lanes = iota((count, 128), 1).astype(F32)
    in_bucket = bucket_col == lanes
    last = jnp.max(jnp.where(in_bucket, iota((count, 128), 0).astype(F32), -1.0), axis=0, keepdims=True)
    last = jnp.where(last < 0, float(count), last)
    label = jnp.max(jnp.where(in_bucket, local_col, -1.0), axis=0, keepdims=True)

    route = fdst[0]
    far_bits = shift_of(far_count)
    to_row = offset_row(lax.shift_right_logical(route, far_bits), me, owners).astype(F32)
    to_col = column(to_row)
    slot_col = column((route & (far_count - 1)).astype(F32))
    f0, f1 = iota((far_count, far_count), 0), iota((far_count, far_count), 1)
    earlier = jnp.where((to_col == to_row) & (f1 < f0), 1.0, 0.0)
    place = to_col * float(depth) + jnp.sum(earlier, axis=1, keepdims=True)
    hit = place == iota((far_count, 128), 1).astype(F32)
    perm = jnp.sum(jnp.where(hit, iota((far_count, 128), 0).astype(F32), 0.0), axis=0, keepdims=True)
    slot = jnp.sum(jnp.where(hit, slot_col + 1.0, 0.0), axis=0, keepdims=True) - 1.0

    tab[PERM : PERM + 1, :] = perm.astype(I32)
    tab[PREV : PREV + 1, 0:count] = prev.astype(I32)
    tab[LAST : LAST + 1, :] = last.astype(I32)
    tab[SLOT : SLOT + 1, :] = slot.astype(I32)
    tab[CLUSTER : CLUSTER + 1, :] = label.astype(I32)
    own_tab = pltpu.make_async_copy(tab, tab_s.at[0], tab_sem.at[0])
    own_tab.start()

    pl.semaphore_wait(barrier, owners - 1 + tgts - 1)

    def send_lab(step):
        return pltpu.make_async_remote_copy(
            src_ref=tab, dst_ref=tab_in.at[step], send_sem=lab_send.at[step],
            recv_sem=lab_recv.at[step], device_id={"src": owner_at(step)}, device_id_type=MESH)

    def send_far(step):
        return pltpu.make_async_remote_copy(
            src_ref=far_out.at[step], dst_ref=far_in.at[step], send_sem=far_send.at[step],
            recv_sem=far_recv.at[step], device_id={"src": owner_at(step)}, device_id_type=MESH)

    def send_near(step):
        return pltpu.make_async_remote_copy(
            src_ref=near_out.at[step], dst_ref=near_in.at[step], send_sem=near_send.at[step],
            recv_sem=near_recv.at[step], device_id={"src": owner_at(step)}, device_id_type=MESH)

    def send_tgt(step):
        return pltpu.make_async_remote_copy(
            src_ref=tg_out.at[step], dst_ref=tg_in.at[step], send_sem=tg_send.at[step],
            recv_sem=tg_recv.at[step], device_id={"tgt": tgt_at(step)}, device_id_type=MESH)

    loop(1, owners, lambda step: send_lab(step).start())

    load_inc.wait()
    for c in range(clusters):
        part = slice(c * PANEL, (c + 1) * PANEL)
        re, im = inc[0, :, part], inc[1, :, part]
        stacked[c, 0:half, 0:PANEL] = re
        stacked[c, 0:half, PANEL:] = -im
        stacked[c, half:, 0:PANEL] = im
        stacked[c, half:, PANEL:] = re
    run[count] = jnp.zeros(run.shape[1:], F32)

    own_tab.wait()
    load_fv.wait()
    lane_item = lax.shift_right_logical(iota((1, width), 1), shift_of(rank))

    def far_step(step):
        picks = [read(0, PERM, step * depth + j, far_count - 1) for j in range(depth)]
        factors = jnp.concatenate(
            [jnp.concatenate([fv[f, 0], fv[f, 1]], axis=1) for f in picks], axis=0)
        source = jnp.zeros((1, width), I32)
        for j, f in enumerate(picks):
            source = jnp.where(lane_item == j, fsrc[0, 0, f], source)
        every = dot_nt(stacked[...].reshape(clusters * 2 * half, 2 * PANEL), factors)
        chosen = every[0 : 2 * half]
        for c in range(1, clusters):
            chosen = jnp.where(source == c, every[c * 2 * half : (c + 1) * 2 * half], chosen)
        return chosen.astype(BF16)

    def far_send_step(step):
        far_out[step] = far_step(step)
        send_far(step).start()

    loop(1, owners, far_send_step)
    far_in[0] = far_step(0)

    @pl.loop(0, count // CHUNK)
    def _(chunk):
        load_nb(chunk).wait()
        for j in range(CHUNK):
            b = chunk * CHUNK + j
            block = jnp.concatenate([nb[b, 0], nb[b, 1]], axis=1)
            product = dot_nt(stacked[nsrc[0, 0, b]], block)
            run[b] = run[read(0, PREV, b, count)] + product

    def near_step(step):
        near_out[step] = run[read(0, LAST, clusters + step - 1, count)].astype(BF16)
        send_near(step).start()

    loop(1, owners, near_step)

    def lab_step(step):
        send_lab(step).wait_recv()
        pltpu.make_async_copy(tab_in.at[step], tab_s.at[step], tab_sem.at[step]).start()

    loop(1, owners, lab_step)
    load_fu.wait()

    def far_apply(step):
        slots = [tab_s[step, SLOT, step * depth + j] for j in range(depth)]
        kept = [jnp.clip(s, 0, far_count - 1) for s in slots]
        factors = jnp.concatenate([fu[s, 0] for s in kept] + [fu[s, 1] for s in kept], axis=0)
        into = jnp.full((1, width), -1, I32)
        for j in range(depth):
            into = jnp.where(lane_item == j, jnp.where(slots[j] < 0, -1, ftgt[0, 0, kept[j]]), into)
        coeff = far_in[step]
        both = jnp.concatenate([coeff, jnp.concatenate([-coeff[half:], coeff[:half]], axis=0)], axis=1)
        into = jnp.concatenate([into, into], axis=1)
        masked = jnp.concatenate(
            [both * jnp.where(into == c, 1.0, 0.0).astype(BF16) for c in range(clusters)], axis=0)
        return jnp.dot(masked, factors, preferred_element_type=F32).reshape(acc.shape)

    total = far_apply(0)
    for c in range(clusters):
        acc[c] = total[c] + run[read(0, LAST, c, count)]

    def far_in_step(step):
        pltpu.make_async_copy(tab_in.at[step], tab_s.at[step], tab_sem.at[step]).wait()
        send_far(step).wait_recv()
        acc[...] += far_apply(step)

    loop(1, owners, far_in_step)

    def near_in_step(step):
        send_near(step).wait_recv()
        where_to = tab_s[step, CLUSTER, clusters + step - 1]
        value = near_in[step].astype(F32)
        for c in range(clusters):
            acc[c] += jnp.where(where_to == c, value, 0.0)

    loop(1, owners, near_in_step)

    for step in range(1, tgts):
        tg_out[step] = acc[pl.ds(tgt_at(step) * share, share)].astype(BF16)
        send_tgt(step).start()
    for step in range(1, tgts):
        send_tgt(step).wait_recv()
    for i in range(share):
        value = acc[mine * share + i]
        for step in range(1, tgts):
            value = value + tg_in[step, i].astype(F32)
        part = slice(i * PANEL, (i + 1) * PANEL)
        out_ref[0, :, part] = value[:half]
        out_ref[1, :, part] = value[half:]

    def drain(step):
        send_lab(step).wait_send()
        send_far(step).wait_send()
        send_near(step).wait_send()

    loop(1, owners, drain)
    for step in range(1, tgts):
        send_tgt(step).wait_send()


def body(incident, near_blocks, near_src, near_tgt, far_v, far_src, far_dst, far_u, far_tgt):
    owners, tgts = lax.axis_size("src"), lax.axis_size("tgt")
    half = incident.shape[1]
    clusters = incident.shape[2] // PANEL
    count, far_count, rank = near_blocks.shape[2], far_v.shape[2], far_v.shape[4]
    depth = max(4, far_count // owners)
    share = clusters // tgts
    rows = 2 * half
    hbm = pl.BlockSpec(memory_space=pltpu.HBM)
    vmem = pl.BlockSpec(memory_space=pltpu.VMEM)
    smem = pl.BlockSpec(memory_space=pltpu.SMEM)
    dma = pltpu.SemaphoreType.DMA
    return pl.pallas_call(
        functools.partial(kernel, owners, tgts, depth),
        out_shape=jax.ShapeDtypeStruct((2, half, share * PANEL), F32),
        in_specs=[hbm, hbm, smem, vmem, hbm, smem, vmem, hbm, smem],
        out_specs=vmem,
        scratch_shapes=[
            pltpu.VMEM(incident.shape, BF16),
            pltpu.VMEM(near_blocks.shape[2:], BF16),
            pltpu.VMEM(far_v.shape[2:], BF16),
            pltpu.VMEM(far_u.shape[2:], BF16),
            pltpu.VMEM((clusters, rows, 2 * PANEL), BF16),
            pltpu.VMEM((8, 128), I32),
            pltpu.VMEM((owners, 8, 128), I32),
            pltpu.SMEM((owners, 8, 128), I32),
            pltpu.VMEM((owners, rows, depth * rank), BF16),
            pltpu.VMEM((owners, rows, depth * rank), BF16),
            pltpu.VMEM((count + 1, rows, PANEL), F32),
            pltpu.VMEM((owners, rows, PANEL), BF16),
            pltpu.VMEM((owners, rows, PANEL), BF16),
            pltpu.VMEM((clusters, rows, PANEL), F32),
            pltpu.VMEM((tgts, share, rows, PANEL), BF16),
            pltpu.VMEM((tgts, share, rows, PANEL), BF16),
            dma((3,)),
            dma((count // CHUNK,)),
            dma((owners,)),
            dma((owners,)), dma((owners,)),
            dma((owners,)), dma((owners,)),
            dma((owners,)), dma((owners,)),
            dma((tgts,)), dma((tgts,)),
        ],
        compiler_params=pltpu.CompilerParams(
            collective_id=0, has_side_effects=True, vmem_limit_bytes=40 * 1024 * 1024),
    )(incident, near_blocks, near_src, near_tgt, far_v, far_src, far_dst, far_u, far_tgt)


def solution(mesh):
    grid = ("groups", "src")
    blocks = P(grid, "tgt", None, None, None, None)
    index = P(grid, "tgt", None)
    return jax.shard_map(
        body,
        mesh=mesh,
        in_specs=(P(None, "dir", grid), blocks, index, index, blocks, index, index, blocks, index),
        out_specs=P(None, "dir", ("groups", "src", "tgt")),
        check_vma=False,
    )
```

```python
import functools

import jax
import jax.numpy as jnp
from jax import lax
from jax.experimental import pallas as pl
from jax.experimental.pallas import tpu as pltpu
from jax.sharding import PartitionSpec as P

PANEL = 128
CHUNK = 8
MESH = pl.DeviceIdType.MESH
F32 = jnp.float32
BF16 = jnp.bfloat16
I32 = jnp.int32

PERM, PREV, LAST, SLOT, CLUSTER = range(5)


def shift_of(size):
    assert size & (size - 1) == 0
    return size.bit_length() - 1


def loop(start, stop, step):
    if stop - start <= 8:
        for index in range(start, stop):
            step(index)
    else:

        @pl.loop(start, stop)
        def _(index):
            step(index)


def iota(shape, axis):
    return lax.broadcasted_iota(I32, shape, axis)


def column(row):
    size = row.shape[1]
    eye = iota((size, size), 0) == iota((size, size), 1)
    return jnp.sum(jnp.where(eye, row, 0.0), axis=1, keepdims=True)


def dot_nt(left, right):
    return lax.dot_general(left, right, (((1,), (1,)), ((), ())), preferred_element_type=F32)


def offset_row(owner, me, owners):
    offset = owner - me
    return jnp.where(offset < 0, offset + owners, offset)


def kernel(
    owners, tgts, depth,
    inc_h, nb_h, nsrc_h, ntgt_h, fv_h, fsrc_h, fdst_h, fu_h, ftgt_h,
    out_ref,
    inc, nb, fv, fu, ntgt, fdst, nsrc, fsrc, ftgt, stacked, tab, tab_in, tab_s, far_out, far_in, run, near_out, near_in, acc,
    tg_out, tg_in,
    in_sem, nb_sem, tab_sem, lab_send, lab_recv, far_send, far_recv, near_send, near_recv,
    tg_send, tg_recv,
):
    count, half = nb.shape[0], inc.shape[1]
    clusters = inc.shape[2] // PANEL
    far_count, rank = fv.shape[0], fv.shape[2]
    width = depth * rank
    share = clusters // tgts
    me, mine = lax.axis_index("src"), lax.axis_index("tgt")

    def read(step, row, lane, top):
        return jnp.clip(tab_s[step, row, lane], 0, top)

    def owner_at(step):
        return lax.rem(me + step, owners)

    def tgt_at(step):
        return lax.rem(mine + step, tgts)

    barrier = pltpu.get_barrier_semaphore()

    def greet_owner(step):
        pl.semaphore_signal(barrier, inc=1, device_id={"src": owner_at(step)}, device_id_type=MESH)

    def greet_tgt(step):
        pl.semaphore_signal(barrier, inc=1, device_id={"tgt": tgt_at(step)}, device_id_type=MESH)

    loop(1, owners, greet_owner)
    loop(1, tgts, greet_tgt)

    load_inc = pltpu.make_async_copy(inc_h.at[...], inc, in_sem.at[0])
    load_fv = pltpu.make_async_copy(fv_h.at[0, 0], fv, in_sem.at[1])
    load_fu = pltpu.make_async_copy(fu_h.at[0, 0], fu, in_sem.at[2])
    load_ntgt = pltpu.make_async_copy(ntgt_h.at[...], ntgt, in_sem.at[3])
    load_fdst = pltpu.make_async_copy(fdst_h.at[...], fdst, in_sem.at[4])
    load_fsrc = pltpu.make_async_copy(fsrc_h.at[...], fsrc, in_sem.at[5])
    load_nsrc = pltpu.make_async_copy(nsrc_h.at[...], nsrc, in_sem.at[6])
    load_ftgt = pltpu.make_async_copy(ftgt_h.at[...], ftgt, in_sem.at[7])
    load_ntgt.start()
    load_fdst.start()
    load_fsrc.start()
    load_inc.start()
    load_fv.start()
    load_nsrc.start()
    load_ftgt.start()

    def load_nb(chunk):
        part = pl.ds(chunk * CHUNK, CHUNK)
        return pltpu.make_async_copy(nb_h.at[0, 0, part], nb.at[part], nb_sem.at[chunk])

    for chunk in range(count // CHUNK):
        load_nb(chunk).start()
    load_fu.start()

    load_ntgt.wait()
    load_fdst.wait()
    target = ntgt[0]
    own_bits = shift_of(clusters)
    step_row = offset_row(lax.shift_right_logical(target, own_bits), me, owners)
    local_row = target & (clusters - 1)
    bucket_row = jnp.where(step_row == 0, local_row, clusters + step_row - 1).astype(F32)
    bucket_col = column(bucket_row)
    local_col = column(local_row.astype(F32))
    at0, at1 = iota((count, count), 0), iota((count, count), 1)
    before = (bucket_col == bucket_row) & (at0 < at1)
    prev = jnp.max(jnp.where(before, at0.astype(F32), -1.0), axis=0, keepdims=True)
    prev = jnp.where(prev < 0, float(count), prev)
    lanes = iota((count, 128), 1).astype(F32)
    in_bucket = bucket_col == lanes
    last = jnp.max(jnp.where(in_bucket, iota((count, 128), 0).astype(F32), -1.0), axis=0, keepdims=True)
    last = jnp.where(last < 0, float(count), last)
    label = jnp.max(jnp.where(in_bucket, local_col, -1.0), axis=0, keepdims=True)

    route = fdst[0]
    far_bits = shift_of(far_count)
    to_row = offset_row(lax.shift_right_logical(route, far_bits), me, owners).astype(F32)
    to_col = column(to_row)
    slot_col = column((route & (far_count - 1)).astype(F32))
    f0, f1 = iota((far_count, far_count), 0), iota((far_count, far_count), 1)
    earlier = jnp.where((to_col == to_row) & (f1 < f0), 1.0, 0.0)
    place = to_col * float(depth) + jnp.sum(earlier, axis=1, keepdims=True)
    hit = place == iota((far_count, 128), 1).astype(F32)
    perm = jnp.sum(jnp.where(hit, iota((far_count, 128), 0).astype(F32), 0.0), axis=0, keepdims=True)
    slot = jnp.sum(jnp.where(hit, slot_col + 1.0, 0.0), axis=0, keepdims=True) - 1.0

    tab[PERM : PERM + 1, :] = perm.astype(I32)
    tab[PREV : PREV + 1, 0:count] = prev.astype(I32)
    tab[LAST : LAST + 1, :] = last.astype(I32)
    tab[SLOT : SLOT + 1, :] = slot.astype(I32)
    tab[CLUSTER : CLUSTER + 1, :] = label.astype(I32)
    own_tab = pltpu.make_async_copy(tab, tab_s.at[0], tab_sem.at[0])
    own_tab.start()

    pl.semaphore_wait(barrier, owners - 1 + tgts - 1)

    def send_lab(step):
        return pltpu.make_async_remote_copy(
            src_ref=tab, dst_ref=tab_in.at[step], send_sem=lab_send.at[step],
            recv_sem=lab_recv.at[step], device_id={"src": owner_at(step)}, device_id_type=MESH)

    def send_far(step):
        return pltpu.make_async_remote_copy(
            src_ref=far_out.at[step], dst_ref=far_in.at[step], send_sem=far_send.at[step],
            recv_sem=far_recv.at[step], device_id={"src": owner_at(step)}, device_id_type=MESH)

    def send_near(step):
        return pltpu.make_async_remote_copy(
            src_ref=near_out.at[step], dst_ref=near_in.at[step], send_sem=near_send.at[step],
            recv_sem=near_recv.at[step], device_id={"src": owner_at(step)}, device_id_type=MESH)

    def send_tgt(step):
        return pltpu.make_async_remote_copy(
            src_ref=tg_out.at[step], dst_ref=tg_in.at[step], send_sem=tg_send.at[step],
            recv_sem=tg_recv.at[step], device_id={"tgt": tgt_at(step)}, device_id_type=MESH)

    loop(1, owners, lambda step: send_lab(step).start())

    load_inc.wait()
    for c in range(clusters):
        part = slice(c * PANEL, (c + 1) * PANEL)
        re, im = inc[0, :, part], inc[1, :, part]
        stacked[c, 0:half, 0:PANEL] = re
        stacked[c, 0:half, PANEL:] = -im
        stacked[c, half:, 0:PANEL] = im
        stacked[c, half:, PANEL:] = re
    run[count] = jnp.zeros(run.shape[1:], F32)

    own_tab.wait()
    load_fsrc.wait()
    load_fv.wait()
    lane_item = lax.shift_right_logical(iota((1, width), 1), shift_of(rank))

    def far_step(step):
        picks = [read(0, PERM, step * depth + j, far_count - 1) for j in range(depth)]
        factors = jnp.concatenate(
            [jnp.concatenate([fv[f, 0], fv[f, 1]], axis=1) for f in picks], axis=0)
        source = jnp.zeros((1, width), I32)
        for j, f in enumerate(picks):
            source = jnp.where(lane_item == j, fsrc[0, 0, f], source)
        every = dot_nt(stacked[...].reshape(clusters * 2 * half, 2 * PANEL), factors)
        chosen = every[0 : 2 * half]
        for c in range(1, clusters):
            chosen = jnp.where(source == c, every[c * 2 * half : (c + 1) * 2 * half], chosen)
        return chosen.astype(BF16)

    def far_send_step(step):
        far_out[step] = far_step(step)
        send_far(step).start()

    loop(1, owners, far_send_step)
    far_in[0] = far_step(0)

    load_nsrc.wait()

    @pl.loop(0, count // CHUNK)
    def _(chunk):
        load_nb(chunk).wait()
        for j in range(CHUNK):
            b = chunk * CHUNK + j
            block = jnp.concatenate([nb[b, 0], nb[b, 1]], axis=1)
            product = dot_nt(stacked[nsrc[0, 0, b]], block)
            run[b] = run[read(0, PREV, b, count)] + product

    def near_step(step):
        near_out[step] = run[read(0, LAST, clusters + step - 1, count)].astype(BF16)
        send_near(step).start()

    loop(1, owners, near_step)

    def lab_step(step):
        send_lab(step).wait_recv()
        pltpu.make_async_copy(tab_in.at[step], tab_s.at[step], tab_sem.at[step]).start()

    loop(1, owners, lab_step)
    load_fu.wait()
    load_ftgt.wait()

    def far_apply(step):
        slots = [tab_s[step, SLOT, step * depth + j] for j in range(depth)]
        kept = [jnp.clip(s, 0, far_count - 1) for s in slots]
        factors = jnp.concatenate([fu[s, 0] for s in kept] + [fu[s, 1] for s in kept], axis=0)
        into = jnp.full((1, width), -1, I32)
        for j in range(depth):
            into = jnp.where(lane_item == j, jnp.where(slots[j] < 0, -1, ftgt[0, 0, kept[j]]), into)
        coeff = far_in[step]
        both = jnp.concatenate([coeff, jnp.concatenate([-coeff[half:], coeff[:half]], axis=0)], axis=1)
        into = jnp.concatenate([into, into], axis=1)
        masked = jnp.concatenate(
            [both * jnp.where(into == c, 1.0, 0.0).astype(BF16) for c in range(clusters)], axis=0)
        return jnp.dot(masked, factors, preferred_element_type=F32).reshape(acc.shape)

    total = far_apply(0)
    for c in range(clusters):
        acc[c] = total[c] + run[read(0, LAST, c, count)]

    def far_in_step(step):
        pltpu.make_async_copy(tab_in.at[step], tab_s.at[step], tab_sem.at[step]).wait()
        send_far(step).wait_recv()
        acc[...] += far_apply(step)

    loop(1, owners, far_in_step)

    def near_in_step(step):
        send_near(step).wait_recv()
        where_to = tab_s[step, CLUSTER, clusters + step - 1]
        value = near_in[step].astype(F32)
        for c in range(clusters):
            acc[c] += jnp.where(where_to == c, value, 0.0)

    loop(1, owners, near_in_step)

    for step in range(1, tgts):
        tg_out[step] = acc[pl.ds(tgt_at(step) * share, share)].astype(BF16)
        send_tgt(step).start()
    for step in range(1, tgts):
        send_tgt(step).wait_recv()
    for i in range(share):
        value = acc[mine * share + i]
        for step in range(1, tgts):
            value = value + tg_in[step, i].astype(F32)
        part = slice(i * PANEL, (i + 1) * PANEL)
        out_ref[0, :, part] = value[:half]
        out_ref[1, :, part] = value[half:]

    def drain(step):
        send_lab(step).wait_send()
        send_far(step).wait_send()
        send_near(step).wait_send()

    loop(1, owners, drain)
    for step in range(1, tgts):
        send_tgt(step).wait_send()


def body(incident, near_blocks, near_src, near_tgt, far_v, far_src, far_dst, far_u, far_tgt):
    owners, tgts = lax.axis_size("src"), lax.axis_size("tgt")
    half = incident.shape[1]
    clusters = incident.shape[2] // PANEL
    count, far_count, rank = near_blocks.shape[2], far_v.shape[2], far_v.shape[4]
    depth = max(4, far_count // owners)
    share = clusters // tgts
    rows = 2 * half
    hbm = pl.BlockSpec(memory_space=pltpu.HBM)
    vmem = pl.BlockSpec(memory_space=pltpu.VMEM)
    dma = pltpu.SemaphoreType.DMA
    return pl.pallas_call(
        functools.partial(kernel, owners, tgts, depth),
        out_shape=jax.ShapeDtypeStruct((2, half, share * PANEL), F32),
        in_specs=[hbm] * 9,
        out_specs=vmem,
        scratch_shapes=[
            pltpu.VMEM(incident.shape, BF16),
            pltpu.VMEM(near_blocks.shape[2:], BF16),
            pltpu.VMEM(far_v.shape[2:], BF16),
            pltpu.VMEM(far_u.shape[2:], BF16),
            pltpu.VMEM(near_tgt.shape, I32),
            pltpu.VMEM(far_dst.shape, I32),
            pltpu.SMEM(near_src.shape, I32),
            pltpu.SMEM(far_src.shape, I32),
            pltpu.SMEM(far_tgt.shape, I32),
            pltpu.VMEM((clusters, rows, 2 * PANEL), BF16),
            pltpu.VMEM((8, 128), I32),
            pltpu.VMEM((owners, 8, 128), I32),
            pltpu.SMEM((owners, 8, 128), I32),
            pltpu.VMEM((owners, rows, depth * rank), BF16),
            pltpu.VMEM((owners, rows, depth * rank), BF16),
            pltpu.VMEM((count + 1, rows, PANEL), F32),
            pltpu.VMEM((owners, rows, PANEL), BF16),
            pltpu.VMEM((owners, rows, PANEL), BF16),
            pltpu.VMEM((clusters, rows, PANEL), F32),
            pltpu.VMEM((tgts, share, rows, PANEL), BF16),
            pltpu.VMEM((tgts, share, rows, PANEL), BF16),
            dma((8,)),
            dma((count // CHUNK,)),
            dma((owners,)),
            dma((owners,)), dma((owners,)),
            dma((owners,)), dma((owners,)),
            dma((owners,)), dma((owners,)),
            dma((tgts,)), dma((tgts,)),
        ],
        compiler_params=pltpu.CompilerParams(
            collective_id=0, has_side_effects=True, vmem_limit_bytes=64 * 1024 * 1024),
    )(incident, near_blocks, near_src, near_tgt, far_v, far_src, far_dst, far_u, far_tgt)


def solution(mesh):
    grid = ("groups", "src")
    blocks = P(grid, "tgt", None, None, None, None)
    index = P(grid, "tgt", None)
    return jax.shard_map(
        body,
        mesh=mesh,
        in_specs=(P(None, "dir", grid), blocks, index, index, blocks, index, index, blocks, index),
        out_specs=P(None, "dir", ("groups", "src", "tgt")),
        check_vma=False,
    )
```

```python
import functools

import jax
import jax.numpy as jnp
from jax import lax
from jax.experimental import pallas as pl
from jax.experimental.pallas import tpu as pltpu
from jax.sharding import PartitionSpec as P

PANEL = 128
CHUNK = 8
MESH = pl.DeviceIdType.MESH
F32 = jnp.float32
BF16 = jnp.bfloat16
I32 = jnp.int32

PERM, PREV, LAST, SLOT, CLUSTER = range(5)


def shift_of(size):
    assert size & (size - 1) == 0
    return size.bit_length() - 1


def loop(start, stop, step):
    if stop - start <= 8:
        for index in range(start, stop):
            step(index)
    else:

        @pl.loop(start, stop)
        def _(index):
            step(index)


def iota(shape, axis):
    return lax.broadcasted_iota(I32, shape, axis)


def column(row):
    size = row.shape[1]
    eye = iota((size, size), 0) == iota((size, size), 1)
    return jnp.sum(jnp.where(eye, row, 0.0), axis=1, keepdims=True)


def dot_nt(left, right):
    return lax.dot_general(left, right, (((1,), (1,)), ((), ())), preferred_element_type=F32)


def offset_row(owner, me, owners):
    offset = owner - me
    return jnp.where(offset < 0, offset + owners, offset)


def kernel(
    owners, tgts, depth,
    inc_h, nb_h, nsrc_h, ntgt_h, fv_h, fsrc_h, fdst_h, fu_h, ftgt_h,
    out_ref,
    inc, nb, fv, fu, ntgt, fdst, nsrc, fsrc, ftgt, stacked, tab, tab_in, tab_s, far_out, far_in, run, near_out, near_in, acc,
    tg_out, tg_in,
    in_sem, nb_sem, tab_sem, lab_send, lab_recv, far_send, far_recv, near_send, near_recv,
    tg_send, tg_recv,
):
    count, half = nb.shape[0], inc.shape[1]
    clusters = inc.shape[2] // PANEL
    far_count, rank = fv.shape[0], fv.shape[2]
    width = depth * rank
    share = clusters // tgts
    me, mine = lax.axis_index("src"), lax.axis_index("tgt")

    def read(step, row, lane, top):
        return jnp.clip(tab_s[step, row, lane], 0, top)

    def owner_at(step):
        return lax.rem(me + step, owners)

    def tgt_at(step):
        return lax.rem(mine + step, tgts)

    barrier = pltpu.get_barrier_semaphore()

    def greet_owner(step):
        pl.semaphore_signal(barrier, inc=1, device_id={"src": owner_at(step)}, device_id_type=MESH)

    def greet_tgt(step):
        pl.semaphore_signal(barrier, inc=1, device_id={"tgt": tgt_at(step)}, device_id_type=MESH)

    loop(1, owners, greet_owner)
    loop(1, tgts, greet_tgt)

    load_inc = pltpu.make_async_copy(inc_h.at[...], inc, in_sem.at[0])
    load_fv = pltpu.make_async_copy(fv_h.at[0, 0], fv, in_sem.at[1])
    load_fu = pltpu.make_async_copy(fu_h.at[0, 0], fu, in_sem.at[2])
    load_ntgt = pltpu.make_async_copy(ntgt_h.at[...], ntgt, in_sem.at[3])
    load_fdst = pltpu.make_async_copy(fdst_h.at[...], fdst, in_sem.at[4])
    load_fsrc = pltpu.make_async_copy(fsrc_h.at[...], fsrc, in_sem.at[5])
    load_nsrc = pltpu.make_async_copy(nsrc_h.at[...], nsrc, in_sem.at[6])
    load_ftgt = pltpu.make_async_copy(ftgt_h.at[...], ftgt, in_sem.at[7])
    load_ntgt.start()
    load_fdst.start()
    load_fsrc.start()
    load_inc.start()
    load_fv.start()
    load_nsrc.start()
    load_ftgt.start()

    def load_nb(chunk):
        part = pl.ds(chunk * CHUNK, CHUNK)
        return pltpu.make_async_copy(nb_h.at[0, 0, part], nb.at[part], nb_sem.at[chunk])

    for chunk in range(count // CHUNK):
        load_nb(chunk).start()
    load_fu.start()

    load_ntgt.wait()
    load_fdst.wait()
    target = ntgt[0]
    own_bits = shift_of(clusters)
    step_row = offset_row(lax.shift_right_logical(target, own_bits), me, owners)
    local_row = target & (clusters - 1)
    bucket_row = jnp.where(step_row == 0, local_row, clusters + step_row - 1).astype(F32)
    bucket_col = column(bucket_row)
    local_col = column(local_row.astype(F32))
    at0, at1 = iota((count, count), 0), iota((count, count), 1)
    before = (bucket_col == bucket_row) & (at0 < at1)
    prev = jnp.max(jnp.where(before, at0.astype(F32), -1.0), axis=0, keepdims=True)
    prev = jnp.where(prev < 0, float(count), prev)
    lanes = iota((count, 128), 1).astype(F32)
    in_bucket = bucket_col == lanes
    last = jnp.max(jnp.where(in_bucket, iota((count, 128), 0).astype(F32), -1.0), axis=0, keepdims=True)
    last = jnp.where(last < 0, float(count), last)
    label = jnp.max(jnp.where(in_bucket, local_col, -1.0), axis=0, keepdims=True)

    route = fdst[0]
    far_bits = shift_of(far_count)
    to_row = offset_row(lax.shift_right_logical(route, far_bits), me, owners).astype(F32)
    to_col = column(to_row)
    slot_col = column((route & (far_count - 1)).astype(F32))
    f0, f1 = iota((far_count, far_count), 0), iota((far_count, far_count), 1)
    earlier = jnp.where((to_col == to_row) & (f1 < f0), 1.0, 0.0)
    place = to_col * float(depth) + jnp.sum(earlier, axis=1, keepdims=True)
    hit = place == iota((far_count, 128), 1).astype(F32)
    perm = jnp.sum(jnp.where(hit, iota((far_count, 128), 0).astype(F32), 0.0), axis=0, keepdims=True)
    slot = jnp.sum(jnp.where(hit, slot_col + 1.0, 0.0), axis=0, keepdims=True) - 1.0

    tab[PERM : PERM + 1, :] = perm.astype(I32)
    tab[PREV : PREV + 1, 0:count] = prev.astype(I32)
    tab[LAST : LAST + 1, :] = last.astype(I32)
    tab[SLOT : SLOT + 1, :] = slot.astype(I32)
    tab[CLUSTER : CLUSTER + 1, :] = label.astype(I32)
    own_tab = pltpu.make_async_copy(tab, tab_s.at[0], tab_sem.at[0])
    own_tab.start()

    pl.semaphore_wait(barrier, owners - 1 + tgts - 1)

    def send_lab(step):
        return pltpu.make_async_remote_copy(
            src_ref=tab, dst_ref=tab_in.at[step], send_sem=lab_send.at[step],
            recv_sem=lab_recv.at[step], device_id={"src": owner_at(step)}, device_id_type=MESH)

    def send_far(step):
        return pltpu.make_async_remote_copy(
            src_ref=far_out.at[step], dst_ref=far_in.at[step], send_sem=far_send.at[step],
            recv_sem=far_recv.at[step], device_id={"src": owner_at(step)}, device_id_type=MESH)

    def send_near(step):
        return pltpu.make_async_remote_copy(
            src_ref=near_out.at[step], dst_ref=near_in.at[step], send_sem=near_send.at[step],
            recv_sem=near_recv.at[step], device_id={"src": owner_at(step)}, device_id_type=MESH)

    def send_tgt(step):
        return pltpu.make_async_remote_copy(
            src_ref=tg_out.at[step], dst_ref=tg_in.at[step], send_sem=tg_send.at[step],
            recv_sem=tg_recv.at[step], device_id={"tgt": tgt_at(step)}, device_id_type=MESH)

    loop(1, owners, lambda step: send_lab(step).start())

    load_inc.wait()
    for c in range(clusters):
        part = slice(c * PANEL, (c + 1) * PANEL)
        re, im = inc[0, :, part], inc[1, :, part]
        stacked[c, 0:half, 0:PANEL] = re
        stacked[c, 0:half, PANEL:] = -im
        stacked[c, half:, 0:PANEL] = im
        stacked[c, half:, PANEL:] = re
    run[count] = jnp.zeros(run.shape[1:], F32)

    own_tab.wait()
    load_fsrc.wait()
    load_fv.wait()
    lane_item = lax.shift_right_logical(iota((1, width), 1), shift_of(rank))

    def far_step(step):
        picks = [read(0, PERM, step * depth + j, far_count - 1) for j in range(depth)]
        factors = jnp.concatenate(
            [jnp.concatenate([fv[f, 0], fv[f, 1]], axis=1) for f in picks], axis=0)
        source = jnp.zeros((1, width), I32)
        for j, f in enumerate(picks):
            source = jnp.where(lane_item == j, fsrc[0, 0, f], source)
        every = dot_nt(stacked[...].reshape(clusters * 2 * half, 2 * PANEL), factors)
        chosen = every[0 : 2 * half]
        for c in range(1, clusters):
            chosen = jnp.where(source == c, every[c * 2 * half : (c + 1) * 2 * half], chosen)
        return chosen.astype(BF16)

    def far_send_step(step):
        far_out[step] = far_step(step)
        send_far(step).start()

    loop(1, owners, far_send_step)
    far_in[0] = far_step(0)

    load_nsrc.wait()

    @pl.loop(0, count // CHUNK)
    def _(chunk):
        load_nb(chunk).wait()
        for j in range(CHUNK):
            b = chunk * CHUNK + j
            block = jnp.concatenate([nb[b, 0], nb[b, 1]], axis=1)
            product = dot_nt(stacked[nsrc[0, 0, b]], block)
            run[b] = run[read(0, PREV, b, count)] + product

    def near_step(step):
        near_out[step] = run[read(0, LAST, clusters + step - 1, count)].astype(BF16)
        send_near(step).start()

    loop(1, owners, near_step)

    def lab_step(step):
        send_lab(step).wait_recv()
        pltpu.make_async_copy(tab_in.at[step], tab_s.at[step], tab_sem.at[step]).start()

    loop(1, owners, lab_step)
    load_fu.wait()
    load_ftgt.wait()

    def far_apply(step):
        slots = [tab_s[step, SLOT, step * depth + j] for j in range(depth)]
        kept = [jnp.clip(s, 0, far_count - 1) for s in slots]
        factors = jnp.concatenate([fu[s, 0] for s in kept] + [fu[s, 1] for s in kept], axis=0)
        into = jnp.full((1, width), -1, I32)
        for j in range(depth):
            into = jnp.where(lane_item == j, jnp.where(slots[j] < 0, -1, ftgt[0, 0, kept[j]]), into)
        coeff = far_in[step]
        both = jnp.concatenate([coeff, jnp.concatenate([-coeff[half:], coeff[:half]], axis=0)], axis=1)
        into = jnp.concatenate([into, into], axis=1)
        masked = jnp.concatenate(
            [both * jnp.where(into == c, 1.0, 0.0).astype(BF16) for c in range(clusters)], axis=0)
        return jnp.dot(masked, factors, preferred_element_type=F32).reshape(acc.shape)

    total = far_apply(0)
    for c in range(clusters):
        acc[c] = total[c] + run[read(0, LAST, c, count)]

    def far_in_step(step):
        pltpu.make_async_copy(tab_in.at[step], tab_s.at[step], tab_sem.at[step]).wait()
        send_far(step).wait_recv()
        acc[...] += far_apply(step)

    loop(1, owners, far_in_step)

    def near_in_step(step):
        send_near(step).wait_recv()
        where_to = tab_s[step, CLUSTER, clusters + step - 1]
        value = near_in[step].astype(F32)
        for c in range(clusters):
            acc[c] += jnp.where(where_to == c, value, 0.0)

    loop(1, owners, near_in_step)

    for step in range(1, tgts):
        tg_out[step] = acc[pl.ds(tgt_at(step) * share, share)].astype(BF16)
        send_tgt(step).start()
    for step in range(1, tgts):
        send_tgt(step).wait_recv()
    for i in range(share):
        value = acc[mine * share + i]
        for step in range(1, tgts):
            value = value + tg_in[step, i].astype(F32)
        part = slice(i * PANEL, (i + 1) * PANEL)
        out_ref[0, :, part] = value[:half]
        out_ref[1, :, part] = value[half:]

    def drain(step):
        send_lab(step).wait_send()
        send_far(step).wait_send()
        send_near(step).wait_send()

    loop(1, owners, drain)
    for step in range(1, tgts):
        send_tgt(step).wait_send()


def body(incident, near_blocks, near_src, near_tgt, far_v, far_src, far_dst, far_u, far_tgt):
    owners, tgts = lax.axis_size("src"), lax.axis_size("tgt")
    half = incident.shape[1]
    clusters = incident.shape[2] // PANEL
    count, far_count, rank = near_blocks.shape[2], far_v.shape[2], far_v.shape[4]
    depth = max(4, far_count // owners)
    share = clusters // tgts
    rows = 2 * half
    hbm = pl.BlockSpec(memory_space=pltpu.HBM)
    vmem = pl.BlockSpec(memory_space=pltpu.VMEM)
    dma = pltpu.SemaphoreType.DMA
    return pl.pallas_call(
        functools.partial(kernel, owners, tgts, depth),
        out_shape=pltpu.VMEM((2, half, share * PANEL), F32),
        in_specs=[hbm] * 9,
        out_specs=vmem,
        scratch_shapes=[
            pltpu.VMEM(incident.shape, BF16),
            pltpu.VMEM(near_blocks.shape[2:], BF16),
            pltpu.VMEM(far_v.shape[2:], BF16),
            pltpu.VMEM(far_u.shape[2:], BF16),
            pltpu.VMEM(near_tgt.shape, I32),
            pltpu.VMEM(far_dst.shape, I32),
            pltpu.SMEM(near_src.shape, I32),
            pltpu.SMEM(far_src.shape, I32),
            pltpu.SMEM(far_tgt.shape, I32),
            pltpu.VMEM((clusters, rows, 2 * PANEL), BF16),
            pltpu.VMEM((8, 128), I32),
            pltpu.VMEM((owners, 8, 128), I32),
            pltpu.SMEM((owners, 8, 128), I32),
            pltpu.VMEM((owners, rows, depth * rank), BF16),
            pltpu.VMEM((owners, rows, depth * rank), BF16),
            pltpu.VMEM((count + 1, rows, PANEL), F32),
            pltpu.VMEM((owners, rows, PANEL), BF16),
            pltpu.VMEM((owners, rows, PANEL), BF16),
            pltpu.VMEM((clusters, rows, PANEL), F32),
            pltpu.VMEM((tgts, share, rows, PANEL), BF16),
            pltpu.VMEM((tgts, share, rows, PANEL), BF16),
            dma((8,)),
            dma((count // CHUNK,)),
            dma((owners,)),
            dma((owners,)), dma((owners,)),
            dma((owners,)), dma((owners,)),
            dma((owners,)), dma((owners,)),
            dma((tgts,)), dma((tgts,)),
        ],
        compiler_params=pltpu.CompilerParams(
            collective_id=0, has_side_effects=True, vmem_limit_bytes=64 * 1024 * 1024 - 131072),
    )(incident, near_blocks, near_src, near_tgt, far_v, far_src, far_dst, far_u, far_tgt)


def solution(mesh):
    grid = ("groups", "src")
    blocks = P(grid, "tgt", None, None, None, None)
    index = P(grid, "tgt", None)
    return jax.shard_map(
        body,
        mesh=mesh,
        in_specs=(P(None, "dir", grid), blocks, index, index, blocks, index, index, blocks, index),
        out_specs=P(None, "dir", ("groups", "src", "tgt")),
        check_vma=False,
    )
```

```python
import functools

import jax
import jax.numpy as jnp
from jax import lax
from jax.experimental import pallas as pl
from jax.experimental.pallas import tpu as pltpu
from jax.sharding import PartitionSpec as P

PANEL = 128
CHUNK = 8
MESH = pl.DeviceIdType.MESH
F32 = jnp.float32
BF16 = jnp.bfloat16
I32 = jnp.int32

PERM, PREV, LAST, SLOT, CLUSTER = range(5)


def shift_of(size):
    assert size & (size - 1) == 0
    return size.bit_length() - 1


def loop(start, stop, step):
    if stop - start <= 8:
        for index in range(start, stop):
            step(index)
    else:

        @pl.loop(start, stop)
        def _(index):
            step(index)


def iota(shape, axis):
    return lax.broadcasted_iota(I32, shape, axis)


def column(row):
    size = row.shape[1]
    eye = iota((size, size), 0) == iota((size, size), 1)
    return jnp.sum(jnp.where(eye, row, 0.0), axis=1, keepdims=True)


def dot_nt(left, right):
    return lax.dot_general(left, right, (((1,), (1,)), ((), ())), preferred_element_type=F32)


def offset_row(owner, me, owners):
    offset = owner - me
    return jnp.where(offset < 0, offset + owners, offset)


def kernel(
    owners, tgts, depth,
    inc_h, nb_h, nsrc_h, ntgt_h, fv_h, fsrc_h, fdst_h, fu_h, ftgt_h,
    out_ref,
    inc, nb, fv, fu, ntgt, fdst, nsrc, fsrc, ftgt, stacked, tab, tab_in, tab_s, far_out, far_in, run, near_out, near_in, acc, acc_near,
    tg_out, tg_in,
    in_sem, nb_sem, tab_sem, lab_send, lab_recv, far_send, far_recv, near_send, near_recv,
    tg_send, tg_recv,
):
    count, half = nb.shape[0], inc.shape[1]
    clusters = inc.shape[2] // PANEL
    far_count, rank = fv.shape[0], fv.shape[2]
    width = depth * rank
    share = clusters // tgts
    me, mine = lax.axis_index("src"), lax.axis_index("tgt")

    def read(step, row, lane, top):
        return jnp.clip(tab_s[step, 0, row, lane], 0, top)

    def owner_at(step):
        return lax.rem(me + step, owners)

    def tgt_at(step):
        return lax.rem(mine + step, tgts)

    barrier = pltpu.get_barrier_semaphore()

    def greet_owner(step):
        for q in range(tgts):
            pl.semaphore_signal(
                barrier, inc=1, device_id={"src": owner_at(step), "tgt": tgt_at(q)},
                device_id_type=MESH)

    def greet_tgt(step):
        pl.semaphore_signal(barrier, inc=1, device_id={"tgt": tgt_at(step)}, device_id_type=MESH)

    loop(1, owners, greet_owner)
    loop(1, tgts, greet_tgt)

    load_inc = pltpu.make_async_copy(inc_h.at[...], inc, in_sem.at[0])
    load_fv = pltpu.make_async_copy(fv_h.at[0, 0], fv, in_sem.at[1])
    load_fu = pltpu.make_async_copy(fu_h.at[0, 0], fu, in_sem.at[2])
    load_ntgt = pltpu.make_async_copy(ntgt_h.at[...], ntgt, in_sem.at[3])
    load_fdst = pltpu.make_async_copy(fdst_h.at[...], fdst, in_sem.at[4])
    load_fsrc = pltpu.make_async_copy(fsrc_h.at[...], fsrc, in_sem.at[5])
    load_nsrc = pltpu.make_async_copy(nsrc_h.at[...], nsrc, in_sem.at[6])
    load_ftgt = pltpu.make_async_copy(ftgt_h.at[...], ftgt, in_sem.at[7])
    load_ntgt.start()
    load_fdst.start()
    load_fsrc.start()
    load_inc.start()
    load_fv.start()
    load_nsrc.start()
    load_ftgt.start()

    def load_nb(chunk):
        part = pl.ds(chunk * CHUNK, CHUNK)
        return pltpu.make_async_copy(nb_h.at[0, 0, part], nb.at[part], nb_sem.at[chunk])

    for chunk in range(count // CHUNK):
        load_nb(chunk).start()
    load_fu.start()

    load_ntgt.wait()
    load_fdst.wait()
    target = ntgt[0]
    own_bits = shift_of(clusters)
    step_row = offset_row(lax.shift_right_logical(target, own_bits), me, owners)
    local_row = target & (clusters - 1)
    bucket_row = jnp.where(step_row == 0, local_row, clusters + step_row - 1).astype(F32)
    bucket_col = column(bucket_row)
    local_col = column(local_row.astype(F32))
    at0, at1 = iota((count, count), 0), iota((count, count), 1)
    before = (bucket_col == bucket_row) & (at0 < at1)
    prev = jnp.max(jnp.where(before, at0.astype(F32), -1.0), axis=0, keepdims=True)
    prev = jnp.where(prev < 0, float(count), prev)
    lanes = iota((count, 128), 1).astype(F32)
    in_bucket = bucket_col == lanes
    last = jnp.max(jnp.where(in_bucket, iota((count, 128), 0).astype(F32), -1.0), axis=0, keepdims=True)
    last = jnp.where(last < 0, float(count), last)
    label = jnp.max(jnp.where(in_bucket, local_col, -1.0), axis=0, keepdims=True)

    route = fdst[0]
    far_bits = shift_of(far_count)
    to_row = offset_row(lax.shift_right_logical(route, far_bits), me, owners).astype(F32)
    to_col = column(to_row)
    slot_col = column((route & (far_count - 1)).astype(F32))
    f0, f1 = iota((far_count, far_count), 0), iota((far_count, far_count), 1)
    earlier = jnp.where((to_col == to_row) & (f1 < f0), 1.0, 0.0)
    place = to_col * float(depth) + jnp.sum(earlier, axis=1, keepdims=True)
    hit = place == iota((far_count, 128), 1).astype(F32)
    perm = jnp.sum(jnp.where(hit, iota((far_count, 128), 0).astype(F32), 0.0), axis=0, keepdims=True)
    slot = jnp.sum(jnp.where(hit, slot_col + 1.0, 0.0), axis=0, keepdims=True) - 1.0

    tab[PERM : PERM + 1, :] = perm.astype(I32)
    tab[PREV : PREV + 1, 0:count] = prev.astype(I32)
    tab[LAST : LAST + 1, :] = last.astype(I32)
    tab[SLOT : SLOT + 1, :] = slot.astype(I32)
    tab[CLUSTER : CLUSTER + 1, :] = label.astype(I32)
    own_tab = pltpu.make_async_copy(tab, tab_s.at[0, 0], tab_sem.at[0, 0])
    own_tab.start()

    pl.semaphore_wait(barrier, owners * tgts - 1)

    def send_lab(step, q):
        return pltpu.make_async_remote_copy(
            src_ref=tab, dst_ref=tab_in.at[step, q], send_sem=lab_send.at[step, q],
            recv_sem=lab_recv.at[step, q],
            device_id={"src": owner_at(step), "tgt": tgt_at(q)}, device_id_type=MESH)

    def send_far(step):
        return pltpu.make_async_remote_copy(
            src_ref=far_out.at[step], dst_ref=far_in.at[step], send_sem=far_send.at[step],
            recv_sem=far_recv.at[step], device_id={"src": owner_at(step)}, device_id_type=MESH)

    def send_near(step, q):
        return pltpu.make_async_remote_copy(
            src_ref=near_out.at[step], dst_ref=near_in.at[step, q], send_sem=near_send.at[step, q],
            recv_sem=near_recv.at[step, q],
            device_id={"src": owner_at(step), "tgt": tgt_at(q)}, device_id_type=MESH)

    def send_tgt(step):
        return pltpu.make_async_remote_copy(
            src_ref=tg_out.at[step], dst_ref=tg_in.at[step], send_sem=tg_send.at[step],
            recv_sem=tg_recv.at[step], device_id={"tgt": tgt_at(step)}, device_id_type=MESH)

    def lab_start(step):
        for q in range(tgts):
            send_lab(step, q).start()

    loop(1, owners, lab_start)

    load_inc.wait()
    for c in range(clusters):
        part = slice(c * PANEL, (c + 1) * PANEL)
        re, im = inc[0, :, part], inc[1, :, part]
        stacked[c, 0:half, 0:PANEL] = re
        stacked[c, 0:half, PANEL:] = -im
        stacked[c, half:, 0:PANEL] = im
        stacked[c, half:, PANEL:] = re
    run[count] = jnp.zeros(run.shape[1:], F32)

    own_tab.wait()
    load_fsrc.wait()
    load_fv.wait()
    lane_item = lax.shift_right_logical(iota((1, width), 1), shift_of(rank))

    def far_step(step):
        picks = [read(0, PERM, step * depth + j, far_count - 1) for j in range(depth)]
        factors = jnp.concatenate(
            [jnp.concatenate([fv[f, 0], fv[f, 1]], axis=1) for f in picks], axis=0)
        source = jnp.zeros((1, width), I32)
        for j, f in enumerate(picks):
            source = jnp.where(lane_item == j, fsrc[0, 0, f], source)
        every = dot_nt(stacked[...].reshape(clusters * 2 * half, 2 * PANEL), factors)
        chosen = every[0 : 2 * half]
        for c in range(1, clusters):
            chosen = jnp.where(source == c, every[c * 2 * half : (c + 1) * 2 * half], chosen)
        return chosen.astype(BF16)

    def far_send_step(step):
        far_out[step] = far_step(step)
        send_far(step).start()

    loop(1, owners, far_send_step)
    far_in[0] = far_step(0)

    load_nsrc.wait()

    @pl.loop(0, count // CHUNK)
    def _(chunk):
        load_nb(chunk).wait()
        for j in range(CHUNK):
            b = chunk * CHUNK + j
            block = jnp.concatenate([nb[b, 0], nb[b, 1]], axis=1)
            product = dot_nt(stacked[nsrc[0, 0, b]], block)
            run[b] = run[read(0, PREV, b, count)] + product

    def near_step(step):
        near_out[step] = run[read(0, LAST, clusters + step - 1, count)].astype(BF16)
        for q in range(tgts):
            send_near(step, q).start()

    loop(1, owners, near_step)

    def load_lab(step, q):
        return pltpu.make_async_copy(tab_in.at[step, q], tab_s.at[step, q], tab_sem.at[step, q])

    def lab_step(step):
        for q in range(tgts):
            send_lab(step, q).wait_recv()
            load_lab(step, q).start()

    loop(1, owners, lab_step)
    load_fu.wait()
    load_ftgt.wait()

    def far_apply(step):
        slots = [tab_s[step, 0, SLOT, step * depth + j] for j in range(depth)]
        kept = [jnp.clip(s, 0, far_count - 1) for s in slots]
        factors = jnp.concatenate([fu[s, 0] for s in kept] + [fu[s, 1] for s in kept], axis=0)
        into = jnp.full((1, width), -1, I32)
        for j in range(depth):
            into = jnp.where(lane_item == j, jnp.where(slots[j] < 0, -1, ftgt[0, 0, kept[j]]), into)
        coeff = far_in[step]
        both = jnp.concatenate([coeff, jnp.concatenate([-coeff[half:], coeff[:half]], axis=0)], axis=1)
        into = jnp.concatenate([into, into], axis=1)
        masked = jnp.concatenate(
            [both * jnp.where(into == c, 1.0, 0.0).astype(BF16) for c in range(clusters)], axis=0)
        return jnp.dot(masked, factors, preferred_element_type=F32).reshape(acc.shape)

    total = far_apply(0)
    for c in range(clusters):
        acc[c] = total[c] + run[read(0, LAST, c, count)]

    def far_in_step(step):
        for q in range(tgts):
            load_lab(step, q).wait()
        send_far(step).wait_recv()
        acc[...] += far_apply(step)

    loop(1, owners, far_in_step)

    for step in range(1, tgts):
        tg_out[step] = acc[pl.ds(tgt_at(step) * share, share)].astype(BF16)
        send_tgt(step).start()

    def near_in_step(step):
        for q in range(tgts):
            send_near(step, q).wait_recv()
            where_to = tab_s[step, q, CLUSTER, clusters + step - 1] - mine * share
            value = near_in[step, q].astype(F32)
            for i in range(share):
                acc_near[i] += jnp.where(where_to == i, value, 0.0)

    for i in range(share):
        acc_near[i] = acc[mine * share + i]
    loop(1, owners, near_in_step)

    for step in range(1, tgts):
        send_tgt(step).wait_recv()
    for i in range(share):
        value = acc_near[i]
        for step in range(1, tgts):
            value = value + tg_in[step, i].astype(F32)
        part = slice(i * PANEL, (i + 1) * PANEL)
        out_ref[0, :, part] = value[:half]
        out_ref[1, :, part] = value[half:]

    def drain(step):
        send_far(step).wait_send()
        for q in range(tgts):
            send_lab(step, q).wait_send()
            send_near(step, q).wait_send()

    loop(1, owners, drain)
    for step in range(1, tgts):
        send_tgt(step).wait_send()


def body(incident, near_blocks, near_src, near_tgt, far_v, far_src, far_dst, far_u, far_tgt):
    owners, tgts = lax.axis_size("src"), lax.axis_size("tgt")
    half = incident.shape[1]
    clusters = incident.shape[2] // PANEL
    count, far_count, rank = near_blocks.shape[2], far_v.shape[2], far_v.shape[4]
    depth = max(4, far_count // owners)
    share = clusters // tgts
    rows = 2 * half
    hbm = pl.BlockSpec(memory_space=pltpu.HBM)
    vmem = pl.BlockSpec(memory_space=pltpu.VMEM)
    dma = pltpu.SemaphoreType.DMA
    return pl.pallas_call(
        functools.partial(kernel, owners, tgts, depth),
        out_shape=pltpu.VMEM((2, half, share * PANEL), F32),
        in_specs=[hbm] * 9,
        out_specs=vmem,
        scratch_shapes=[
            pltpu.VMEM(incident.shape, BF16),
            pltpu.VMEM(near_blocks.shape[2:], BF16),
            pltpu.VMEM(far_v.shape[2:], BF16),
            pltpu.VMEM(far_u.shape[2:], BF16),
            pltpu.VMEM(near_tgt.shape, I32),
            pltpu.VMEM(far_dst.shape, I32),
            pltpu.SMEM(near_src.shape, I32),
            pltpu.SMEM(far_src.shape, I32),
            pltpu.SMEM(far_tgt.shape, I32),
            pltpu.VMEM((clusters, rows, 2 * PANEL), BF16),
            pltpu.VMEM((8, 128), I32),
            pltpu.VMEM((owners, tgts, 8, 128), I32),
            pltpu.SMEM((owners, tgts, 8, 128), I32),
            pltpu.VMEM((owners, rows, depth * rank), BF16),
            pltpu.VMEM((owners, rows, depth * rank), BF16),
            pltpu.VMEM((count + 1, rows, PANEL), F32),
            pltpu.VMEM((owners, rows, PANEL), BF16),
            pltpu.VMEM((owners, tgts, rows, PANEL), BF16),
            pltpu.VMEM((clusters, rows, PANEL), F32),
            pltpu.VMEM((share, rows, PANEL), F32),
            pltpu.VMEM((tgts, share, rows, PANEL), BF16),
            pltpu.VMEM((tgts, share, rows, PANEL), BF16),
            dma((8,)),
            dma((count // CHUNK,)),
            dma((owners, tgts)),
            dma((owners, tgts)), dma((owners, tgts)),
            dma((owners,)), dma((owners,)),
            dma((owners, tgts)), dma((owners, tgts)),
            dma((tgts,)), dma((tgts,)),
        ],
        compiler_params=pltpu.CompilerParams(
            collective_id=0, has_side_effects=True, vmem_limit_bytes=64 * 1024 * 1024 - 131072),
    )(incident, near_blocks, near_src, near_tgt, far_v, far_src, far_dst, far_u, far_tgt)


def solution(mesh):
    grid = ("groups", "src")
    blocks = P(grid, "tgt", None, None, None, None)
    index = P(grid, "tgt", None)
    return jax.shard_map(
        body,
        mesh=mesh,
        in_specs=(P(None, "dir", grid), blocks, index, index, blocks, index, index, blocks, index),
        out_specs=P(None, "dir", ("groups", "src", "tgt")),
        check_vma=False,
    )
```

```python
import functools

import jax
import jax.numpy as jnp
from jax import lax
from jax.experimental import pallas as pl
from jax.experimental.pallas import tpu as pltpu
from jax.sharding import PartitionSpec as P

PANEL = 128
CHUNK = 8
MESH = pl.DeviceIdType.MESH
F32 = jnp.float32
BF16 = jnp.bfloat16
I32 = jnp.int32

PERM, PREV, LAST, SLOT, CLUSTER = range(5)


def shift_of(size):
    assert size & (size - 1) == 0
    return size.bit_length() - 1


def loop(start, stop, step):
    if stop - start <= 8:
        for index in range(start, stop):
            step(index)
    else:

        @pl.loop(start, stop)
        def _(index):
            step(index)


def iota(shape, axis):
    return lax.broadcasted_iota(I32, shape, axis)


def column(row):
    size = row.shape[1]
    eye = iota((size, size), 0) == iota((size, size), 1)
    return jnp.sum(jnp.where(eye, row, 0.0), axis=1, keepdims=True)


def dot_nt(left, right):
    return lax.dot_general(left, right, (((1,), (1,)), ((), ())), preferred_element_type=F32)


def offset_row(owner, me, owners):
    offset = owner - me
    return jnp.where(offset < 0, offset + owners, offset)


def kernel(
    owners, tgts, depth,
    inc_h, nb_h, nsrc_h, ntgt_h, fv_h, fsrc_h, fdst_h, fu_h, ftgt_h,
    out_ref,
    inc, nb, fv, fu, ntgt, fdst, nsrc, fsrc, ftgt, stacked, tab, tab_in, tab_s, far_out, far_in, run, near_out, near_in, acc, acc_near,
    tg_out, tg_in,
    in_sem, nb_sem, tab_sem, lab_send, lab_recv, far_send, far_recv, near_send, near_recv,
    tg_send, tg_recv,
):
    count, half = nb.shape[0], inc.shape[1]
    clusters = inc.shape[2] // PANEL
    far_count, rank = fv.shape[0], fv.shape[2]
    width = depth * rank
    share = clusters // tgts
    me, mine = lax.axis_index("src"), lax.axis_index("tgt")

    def read(step, row, lane, top):
        return jnp.clip(tab_s[step, 0, row, lane], 0, top)

    def owner_at(step):
        return lax.rem(me + step, owners)

    def tgt_at(step):
        return lax.rem(mine + step, tgts)

    barrier = pltpu.get_barrier_semaphore()

    def greet_owner(step):
        for q in range(tgts):
            pl.semaphore_signal(
                barrier, inc=1, device_id={"src": owner_at(step), "tgt": tgt_at(q)},
                device_id_type=MESH)

    def greet_tgt(step):
        pl.semaphore_signal(barrier, inc=1, device_id={"tgt": tgt_at(step)}, device_id_type=MESH)

    loop(1, owners, greet_owner)
    loop(1, tgts, greet_tgt)

    load_inc = pltpu.make_async_copy(inc_h.at[...], inc, in_sem.at[0])
    load_fv = pltpu.make_async_copy(fv_h.at[0, 0], fv, in_sem.at[1])
    load_fu = pltpu.make_async_copy(fu_h.at[0, 0], fu, in_sem.at[2])
    load_ntgt = pltpu.make_async_copy(ntgt_h.at[...], ntgt, in_sem.at[3])
    load_fdst = pltpu.make_async_copy(fdst_h.at[...], fdst, in_sem.at[4])
    load_fsrc = pltpu.make_async_copy(fsrc_h.at[...], fsrc, in_sem.at[5])
    load_nsrc = pltpu.make_async_copy(nsrc_h.at[...], nsrc, in_sem.at[6])
    load_ftgt = pltpu.make_async_copy(ftgt_h.at[...], ftgt, in_sem.at[7])
    load_ntgt.start()
    load_fdst.start()
    load_fsrc.start()
    load_inc.start()
    load_fv.start()
    load_nsrc.start()
    load_ftgt.start()

    def load_nb(chunk):
        part = pl.ds(chunk * CHUNK, CHUNK)
        return pltpu.make_async_copy(nb_h.at[0, 0, part], nb.at[part], nb_sem.at[chunk])

    for chunk in range(count // CHUNK):
        load_nb(chunk).start()
    load_fu.start()

    load_ntgt.wait()
    load_fdst.wait()
    target = ntgt[0]
    own_bits = shift_of(clusters)
    step_row = offset_row(lax.shift_right_logical(target, own_bits), me, owners)
    local_row = target & (clusters - 1)
    bucket_row = jnp.where(step_row == 0, local_row, clusters + step_row - 1).astype(F32)
    bucket_col = column(bucket_row)
    local_col = column(local_row.astype(F32))
    at0, at1 = iota((count, count), 0), iota((count, count), 1)
    before = (bucket_col == bucket_row) & (at0 < at1)
    prev = jnp.max(jnp.where(before, at0.astype(F32), -1.0), axis=0, keepdims=True)
    prev = jnp.where(prev < 0, float(count), prev)
    lanes = iota((count, 128), 1).astype(F32)
    in_bucket = bucket_col == lanes
    last = jnp.max(jnp.where(in_bucket, iota((count, 128), 0).astype(F32), -1.0), axis=0, keepdims=True)
    last = jnp.where(last < 0, float(count), last)
    label = jnp.max(jnp.where(in_bucket, local_col, -1.0), axis=0, keepdims=True)

    route = fdst[0]
    far_bits = shift_of(far_count)
    to_row = offset_row(lax.shift_right_logical(route, far_bits), me, owners).astype(F32)
    to_col = column(to_row)
    slot_col = column((route & (far_count - 1)).astype(F32))
    f0, f1 = iota((far_count, far_count), 0), iota((far_count, far_count), 1)
    earlier = jnp.where((to_col == to_row) & (f1 < f0), 1.0, 0.0)
    place = to_col * float(depth) + jnp.sum(earlier, axis=1, keepdims=True)
    hit = place == iota((far_count, 128), 1).astype(F32)
    perm = jnp.sum(jnp.where(hit, iota((far_count, 128), 0).astype(F32), 0.0), axis=0, keepdims=True)
    slot = jnp.sum(jnp.where(hit, slot_col + 1.0, 0.0), axis=0, keepdims=True) - 1.0

    tab[PERM : PERM + 1, :] = perm.astype(I32)
    tab[PREV : PREV + 1, 0:count] = prev.astype(I32)
    tab[LAST : LAST + 1, :] = last.astype(I32)
    tab[SLOT : SLOT + 1, :] = slot.astype(I32)
    tab[CLUSTER : CLUSTER + 1, :] = label.astype(I32)
    own_tab = pltpu.make_async_copy(tab, tab_s.at[0, 0], tab_sem.at[0, 0])
    own_tab.start()

    pl.semaphore_wait(barrier, owners * tgts - 1)

    def send_lab(step, q):
        return pltpu.make_async_remote_copy(
            src_ref=tab, dst_ref=tab_in.at[step, q], send_sem=lab_send.at[step, q],
            recv_sem=lab_recv.at[step, q],
            device_id={"src": owner_at(step), "tgt": tgt_at(q)}, device_id_type=MESH)

    def send_far(step):
        return pltpu.make_async_remote_copy(
            src_ref=far_out.at[step], dst_ref=far_in.at[step], send_sem=far_send.at[step],
            recv_sem=far_recv.at[step], device_id={"src": owner_at(step)}, device_id_type=MESH)

    def send_near(step, q):
        return pltpu.make_async_remote_copy(
            src_ref=near_out.at[step], dst_ref=near_in.at[step, q], send_sem=near_send.at[step, q],
            recv_sem=near_recv.at[step, q],
            device_id={"src": owner_at(step), "tgt": tgt_at(q)}, device_id_type=MESH)

    def send_tgt(step):
        return pltpu.make_async_remote_copy(
            src_ref=tg_out.at[step], dst_ref=tg_in.at[step], send_sem=tg_send.at[step],
            recv_sem=tg_recv.at[step], device_id={"tgt": tgt_at(step)}, device_id_type=MESH)

    def lab_start(step):
        send_lab(step, 0).start()

    def near_lab_start(step):
        for q in range(1, tgts):
            send_lab(step, q).start()

    loop(1, owners, lab_start)

    load_inc.wait()
    for c in range(clusters):
        part = slice(c * PANEL, (c + 1) * PANEL)
        re, im = inc[0, :, part], inc[1, :, part]
        stacked[c, 0:half, 0:PANEL] = re
        stacked[c, 0:half, PANEL:] = -im
        stacked[c, half:, 0:PANEL] = im
        stacked[c, half:, PANEL:] = re
    run[count] = jnp.zeros(run.shape[1:], F32)

    own_tab.wait()
    load_fsrc.wait()
    load_fv.wait()
    lane_item = lax.shift_right_logical(iota((1, width), 1), shift_of(rank))

    def far_step(step):
        picks = [read(0, PERM, step * depth + j, far_count - 1) for j in range(depth)]
        factors = jnp.concatenate(
            [jnp.concatenate([fv[f, 0], fv[f, 1]], axis=1) for f in picks], axis=0)
        source = jnp.zeros((1, width), I32)
        for j, f in enumerate(picks):
            source = jnp.where(lane_item == j, fsrc[0, 0, f], source)
        every = dot_nt(stacked[...].reshape(clusters * 2 * half, 2 * PANEL), factors)
        chosen = every[0 : 2 * half]
        for c in range(1, clusters):
            chosen = jnp.where(source == c, every[c * 2 * half : (c + 1) * 2 * half], chosen)
        return chosen.astype(BF16)

    def far_send_step(step):
        far_out[step] = far_step(step)
        send_far(step).start()

    loop(1, owners, far_send_step)
    loop(1, owners, near_lab_start)
    far_in[0] = far_step(0)

    load_nsrc.wait()

    @pl.loop(0, count // CHUNK)
    def _(chunk):
        load_nb(chunk).wait()
        for j in range(CHUNK):
            b = chunk * CHUNK + j
            block = jnp.concatenate([nb[b, 0], nb[b, 1]], axis=1)
            product = dot_nt(stacked[nsrc[0, 0, b]], block)
            run[b] = run[read(0, PREV, b, count)] + product

    def near_step(step):
        near_out[step] = run[read(0, LAST, clusters + step - 1, count)].astype(BF16)
        for q in reversed(range(tgts)):
            send_near(step, q).start()

    loop(1, owners, near_step)

    def load_lab(step, q):
        return pltpu.make_async_copy(tab_in.at[step, q], tab_s.at[step, q], tab_sem.at[step, q])

    def lab_step(step):
        send_lab(step, 0).wait_recv()
        load_lab(step, 0).start()

    loop(1, owners, lab_step)
    load_fu.wait()
    load_ftgt.wait()

    def far_apply(step):
        slots = [tab_s[step, 0, SLOT, step * depth + j] for j in range(depth)]
        kept = [jnp.clip(s, 0, far_count - 1) for s in slots]
        factors = jnp.concatenate([fu[s, 0] for s in kept] + [fu[s, 1] for s in kept], axis=0)
        into = jnp.full((1, width), -1, I32)
        for j in range(depth):
            into = jnp.where(lane_item == j, jnp.where(slots[j] < 0, -1, ftgt[0, 0, kept[j]]), into)
        coeff = far_in[step]
        both = jnp.concatenate([coeff, jnp.concatenate([-coeff[half:], coeff[:half]], axis=0)], axis=1)
        into = jnp.concatenate([into, into], axis=1)
        masked = jnp.concatenate(
            [both * jnp.where(into == c, 1.0, 0.0).astype(BF16) for c in range(clusters)], axis=0)
        return jnp.dot(masked, factors, preferred_element_type=F32).reshape(acc.shape)

    total = far_apply(0)
    for c in range(clusters):
        acc[c] = total[c] + run[read(0, LAST, c, count)]

    def far_in_step(step):
        load_lab(step, 0).wait()
        send_far(step).wait_recv()
        acc[...] += far_apply(step)

    loop(1, owners, far_in_step)

    for step in range(1, tgts):
        tg_out[step] = acc[pl.ds(tgt_at(step) * share, share)].astype(BF16)
        send_tgt(step).start()

    def near_lab_step(step):
        for q in range(1, tgts):
            send_lab(step, q).wait_recv()
            load_lab(step, q).start()

    loop(1, owners, near_lab_step)

    def near_in_step(step):
        for q in range(tgts):
            if q:
                load_lab(step, q).wait()
            send_near(step, q).wait_recv()
            where_to = tab_s[step, q, CLUSTER, clusters + step - 1] - mine * share
            value = near_in[step, q].astype(F32)
            for i in range(share):
                acc_near[i] += jnp.where(where_to == i, value, 0.0)

    for i in range(share):
        acc_near[i] = acc[mine * share + i]
    loop(1, owners, near_in_step)

    for step in range(1, tgts):
        send_tgt(step).wait_recv()
    for i in range(share):
        value = acc_near[i]
        for step in range(1, tgts):
            value = value + tg_in[step, i].astype(F32)
        part = slice(i * PANEL, (i + 1) * PANEL)
        out_ref[0, :, part] = value[:half]
        out_ref[1, :, part] = value[half:]

    def drain(step):
        send_far(step).wait_send()
        for q in range(tgts):
            send_lab(step, q).wait_send()
            send_near(step, q).wait_send()

    loop(1, owners, drain)
    for step in range(1, tgts):
        send_tgt(step).wait_send()


def body(incident, near_blocks, near_src, near_tgt, far_v, far_src, far_dst, far_u, far_tgt):
    owners, tgts = lax.axis_size("src"), lax.axis_size("tgt")
    half = incident.shape[1]
    clusters = incident.shape[2] // PANEL
    count, far_count, rank = near_blocks.shape[2], far_v.shape[2], far_v.shape[4]
    depth = max(4, far_count // owners)
    share = clusters // tgts
    rows = 2 * half
    hbm = pl.BlockSpec(memory_space=pltpu.HBM)
    vmem = pl.BlockSpec(memory_space=pltpu.VMEM)
    dma = pltpu.SemaphoreType.DMA
    return pl.pallas_call(
        functools.partial(kernel, owners, tgts, depth),
        out_shape=pltpu.VMEM((2, half, share * PANEL), F32),
        in_specs=[hbm] * 9,
        out_specs=vmem,
        scratch_shapes=[
            pltpu.VMEM(incident.shape, BF16),
            pltpu.VMEM(near_blocks.shape[2:], BF16),
            pltpu.VMEM(far_v.shape[2:], BF16),
            pltpu.VMEM(far_u.shape[2:], BF16),
            pltpu.VMEM(near_tgt.shape, I32),
            pltpu.VMEM(far_dst.shape, I32),
            pltpu.SMEM(near_src.shape, I32),
            pltpu.SMEM(far_src.shape, I32),
            pltpu.SMEM(far_tgt.shape, I32),
            pltpu.VMEM((clusters, rows, 2 * PANEL), BF16),
            pltpu.VMEM((8, 128), I32),
            pltpu.VMEM((owners, tgts, 8, 128), I32),
            pltpu.SMEM((owners, tgts, 8, 128), I32),
            pltpu.VMEM((owners, rows, depth * rank), BF16),
            pltpu.VMEM((owners, rows, depth * rank), BF16),
            pltpu.VMEM((count + 1, rows, PANEL), F32),
            pltpu.VMEM((owners, rows, PANEL), BF16),
            pltpu.VMEM((owners, tgts, rows, PANEL), BF16),
            pltpu.VMEM((clusters, rows, PANEL), F32),
            pltpu.VMEM((share, rows, PANEL), F32),
            pltpu.VMEM((tgts, share, rows, PANEL), BF16),
            pltpu.VMEM((tgts, share, rows, PANEL), BF16),
            dma((8,)),
            dma((count // CHUNK,)),
            dma((owners, tgts)),
            dma((owners, tgts)), dma((owners, tgts)),
            dma((owners,)), dma((owners,)),
            dma((owners, tgts)), dma((owners, tgts)),
            dma((tgts,)), dma((tgts,)),
        ],
        compiler_params=pltpu.CompilerParams(
            collective_id=0, has_side_effects=True, vmem_limit_bytes=64 * 1024 * 1024 - 131072),
    )(incident, near_blocks, near_src, near_tgt, far_v, far_src, far_dst, far_u, far_tgt)


def solution(mesh):
    grid = ("groups", "src")
    blocks = P(grid, "tgt", None, None, None, None)
    index = P(grid, "tgt", None)
    return jax.shard_map(
        body,
        mesh=mesh,
        in_specs=(P(None, "dir", grid), blocks, index, index, blocks, index, index, blocks, index),
        out_specs=P(None, "dir", ("groups", "src", "tgt")),
        check_vma=False,
    )
```
